32 devices in a mesh: groups: 2 (over y), lon: 4 (over z), lat: 2 (over x), sub: 2 (over core).
Axes of the slice: x: 2, y: 2, z: 4, core: 2. Of those that a mesh axis runs over, the one named last changes fastest.
Arguments:
- tokens: bfloat16 [512, 200, 384], P(('groups', 'lat', 'lon')), parts along dimension 0, may hold values from -130 to 130, as said below
- land_bits: int32 [512, 200], P(('groups', 'lat', 'lon')), parts along dimension 0, may hold values from 0 to 1, as said below
- ocean_list: int32 [4, 128], P(('groups', 'lat')), parts along dimension 0, may hold values from 0 to 128, as said below
- w_qkv: bfloat16 [2, 3, 384, 384], P(None, None, None, 'sub'), as said below
- w_out: bfloat16 [2, 384, 384], P(None, 'sub'), may hold values from -0.3125 to 0.3125
Outputs:
- advanced: bfloat16 [512, 200, 384], P(('groups', 'lat', 'lon')), parts along dimension 0
The draws below stay inside these ranges and needn't reach their ends.
There are 2 independent parts, one for each index of `groups`. The reference program is written for one: setup_inputs(seed, part) draws one part's arguments, and reference() takes and returns one part's arrays. A program takes and returns all parts, laid end to end along the dimension named above; an argument that names none is the same for every part. Nothing has to cross between parts.
Inputs may be any that keep to these rules, and one draw needn't show every extreme that they name: `ocean_list`: each row lists its band's ocean windows in increasing order and then holds 128. A row lists at least 72 and at most 96 windows; some row lists exactly 96. In each window row of a band the listed windows form one run along longitude, which may wrap around. `land_bits`: every token of a window that its band's row of ocean_list does not list is land; in listed windows about a quarter of the tokens are land. `tokens`: finite values. `w_qkv`: entries lie within 165 / sqrt(384) in magnitude.
All inputs are finite; a program needn't handle non-finite values.
Results may differ from the reference program's by a relative error of at most 0.013.
Values may be sent and summed in bfloat16 or wider, within the bound.
A program may use at most 64 MiB of HBM per device.

```python
import jax
import jax.numpy as jnp
from jax import lax

D = 384
HEADS = 12
HD = 32
HGROUPS = 2
WH = 10
WW = 20
P_SIZE = 200
LONW = 32
WROW_DEV = 4
BANDS = 2
LATW = 8
BAND_WINDOWS = 128
WINDOWS = 256
OCEAN_MOST = 96
NLAT = 80
NLON = 640


def ocean_layout(key):
    seeds = jax.random.split(jax.random.fold_in(key, 31), 4)
    shortfall = jax.random.randint(seeds[0], (BANDS,), 0, OCEAN_MOST // 4 + 1)
    fullest = jax.random.randint(seeds[1], (), 0, BANDS)
    band_index = jnp.arange(BANDS, dtype=jnp.int32)
    ocean_count = jnp.where(band_index == fullest, OCEAN_MOST, OCEAN_MOST - shortfall)
    row_index = jnp.arange(WROW_DEV, dtype=jnp.int32)[None, :]
    row_count = ocean_count[:, None] // WROW_DEV + (row_index < ocean_count[:, None] % WROW_DEV).astype(jnp.int32)
    offset = jax.random.randint(seeds[2], (BANDS, WROW_DEV, 1), 0, LONW)
    column = jnp.arange(LONW, dtype=jnp.int32)[None, None, :]
    is_ocean = (column - offset) % LONW < row_count[:, :, None]
    local = jnp.swapaxes(is_ocean, 1, 2).reshape(BANDS, BAND_WINDOWS)
    return (local, ocean_count, seeds[3])


def draw_ocean_list(key, part):
    local, ocean_count, unused = ocean_layout(key)
    window_index = jnp.broadcast_to(jnp.arange(BAND_WINDOWS, dtype=jnp.int32)[None, :], (BANDS, BAND_WINDOWS))
    ordering = jnp.where(local, window_index, window_index + BAND_WINDOWS)
    ranked = jnp.sort(ordering, axis=1)
    position = jnp.arange(BAND_WINDOWS, dtype=jnp.int32)[None, :]
    return jnp.where(position < ocean_count[:, None], ranked, BAND_WINDOWS).astype(jnp.int32)


def draw_land_bits(key, part):
    local, ocean_count, coast_key = ocean_layout(key)
    window_ocean = local.reshape(WINDOWS)
    coastal = jax.random.randint(coast_key, (WINDOWS, P_SIZE), 0, 4) == 0
    return jnp.where(window_ocean[:, None], coastal, True).astype(jnp.int32)


def draw_tokens(key, part):
    seeds = jax.random.split(jax.random.fold_in(key, 11), 1)
    drawn = jnp.clip(jax.random.normal(seeds[0], (WINDOWS, P_SIZE, D)), -6.0, 6.0)
    return drawn.astype(jnp.bfloat16)


def draw_w_qkv(key, part):
    seeds = jax.random.split(jax.random.fold_in(key, 23), 1)
    raw = jnp.clip(jax.random.normal(seeds[0], (2, 3, D, D)), -6.0, 6.0) * D ** (-0.5)
    factor = jnp.array([1.7, 1.7, 1.0], dtype=jnp.float32)[None, :, None, None]
    weights = raw * factor
    return weights.astype(jnp.bfloat16)


def levels(key, dims, shards, least, largest):
    gain, own = 1.0, jax.random.fold_in(key, 6)
    for axis_at, blocks in shards:
        draws = jnp.exp(jax.random.uniform(jax.random.fold_in(own, axis_at), (blocks,), jnp.float32, least / len(shards), largest / len(shards)))
        gain = gain * jnp.repeat(draws, dims[axis_at] // blocks).reshape([-1 if axis == axis_at else 1 for axis in range(len(dims))])
    return gain


def gaussian(key, extent, width, bound, cuts=(), kind=jnp.bfloat16):
    values = width * jax.random.normal(key, extent, jnp.float32)
    if cuts:
        values = values * levels(key, extent, cuts, -0.22, 0.18)
    return jnp.clip(values, -bound, bound).astype(kind)


def setup_inputs(seed: int = 0, part: int = 0) -> dict:
    keys = jax.random.split(jax.random.key(seed), 6)
    part_keys = jax.random.split(jax.random.fold_in(keys[5], part), 6)
    tokens = draw_tokens(jax.random.fold_in(jax.random.fold_in(keys[5], part), 71), part)
    land_bits = draw_land_bits(jax.random.fold_in(jax.random.fold_in(keys[5], part), 71), part)
    ocean_list = draw_ocean_list(jax.random.fold_in(jax.random.fold_in(keys[5], part), 71), part)
    w_qkv = draw_w_qkv(jax.random.fold_in(keys[5], 71), part)
    w_out = gaussian(keys[4], (2, D, D), D ** -0.5, 0.3125, ((1, 2),))
    return {"tokens": tokens, "land_bits": land_bits, "ocean_list": ocean_list, "w_qkv": w_qkv, "w_out": w_out}


def layer_normal(values):
    center = lax.optimization_barrier(jnp.mean(values, axis=-1, keepdims=True))
    centred = values - center
    variance = lax.optimization_barrier(jnp.mean(centred * centred, axis=-1, keepdims=True))
    return centred * lax.rsqrt(variance + 1e-05)

def rounded(values):
    return lax.optimization_barrier(values.astype(jnp.bfloat16)).astype(jnp.float32)

def window_terms(windows, land_keys, w_qkv_block, w_out_block):
    window_count = windows.shape[0]
    normed = rounded(layer_normal(windows.astype(jnp.float32)))

    def project(which_part):
        product = jnp.einsum('wpd,de->wpe', normed, w_qkv_block[which_part].astype(jnp.float32))
        return rounded(product).reshape(window_count, P_SIZE, HEADS, HD)
    query = project(0)
    keyed = project(1)
    valued = project(2)
    scores = jnp.einsum('wphe,wkhe->whpk', query, keyed) * HD ** (-0.5)
    scores = jnp.where(land_keys[:, None, None, :] > 0, -1e+30, scores)
    highest = lax.optimization_barrier(jnp.max(scores, axis=-1, keepdims=True))
    powers = jnp.exp(scores - highest)
    probs = rounded(powers / lax.optimization_barrier(jnp.sum(powers, axis=-1, keepdims=True)))
    blended = rounded(jnp.einsum('whpk,wkhe->wphe', probs, valued).reshape(window_count, P_SIZE, D))
    group_width = D // HGROUPS
    update = jnp.zeros((window_count, P_SIZE, D), jnp.float32)
    for group in range(HGROUPS):
        lower = group * group_width
        partial_value = jnp.einsum('wpe,ed->wpd', blended[:, :, lower:lower + group_width], w_out_block[lower:lower + group_width].astype(jnp.float32))
        update = update + rounded(partial_value)
    return update

def to_grid(windows):
    tail = windows.shape[2:]
    split = windows.reshape((BANDS, LONW, WROW_DEV, WH, WW) + tail)
    moved = jnp.transpose(split, (0, 2, 3, 1, 4) + tuple(range(5, 5 + len(tail))))
    return moved.reshape((NLAT, NLON) + tail)

def from_grid(image):
    tail = image.shape[2:]
    split = image.reshape((BANDS, WROW_DEV, WH, LONW, WW) + tail)
    moved = jnp.transpose(split, (0, 3, 1, 2, 4) + tuple(range(5, 5 + len(tail))))
    return moved.reshape((WINDOWS, P_SIZE) + tail)

def to_windows(image):
    tail = image.shape[2:]
    split = image.reshape((LATW, WH, LONW, WW) + tail)
    moved = jnp.swapaxes(split, 1, 2)
    return moved.reshape((LATW * LONW, P_SIZE) + tail)

def from_windows(windows):
    tail = windows.shape[2:]
    split = windows.reshape((LATW, LONW, WH, WW) + tail)
    return jnp.swapaxes(split, 1, 2).reshape((NLAT, NLON) + tail)

def apply_block(image, land, active, w_qkv_block, w_out_block):
    windows = to_windows(image)
    land_windows = to_windows(land)
    grouped = windows.reshape(LATW, LONW, P_SIZE, D)
    grouped_land = land_windows.reshape(LATW, LONW, P_SIZE)

    def inner(packed):
        return window_terms(packed[0], packed[1], w_qkv_block, w_out_block)
    updates = lax.map(inner, (grouped, grouped_land)).reshape(LATW * LONW, P_SIZE, D)
    ocean = 1.0 - land_windows.astype(jnp.float32)
    keeping = (active.reshape(LATW * LONW, 1).astype(jnp.float32) * ocean)[:, :, None]
    result = (windows.astype(jnp.float32) + updates * keeping).astype(jnp.bfloat16)
    return from_windows(result)

def reference(tokens, land_bits, ocean_list, w_qkv, w_out):
    grid = to_grid(tokens)
    land_grid = to_grid(land_bits)
    band_index = jnp.arange(BAND_WINDOWS, dtype=jnp.int32)
    listed_local = jnp.any(ocean_list[:, :, None] == band_index[None, None, :], axis=1)
    listed = jnp.swapaxes(listed_local.reshape(BANDS, LONW, WROW_DEV), 1, 2).reshape(LATW, LONW)
    first = apply_block(grid, land_grid, listed, w_qkv[0], w_out[0])
    half_rows = WH // 2
    half_cols = WW // 2
    rolled = jnp.roll(first, (-half_rows, -half_cols), axis=(0, 1))
    rolled_land = jnp.roll(land_grid, (-half_rows, -half_cols), axis=(0, 1))
    valid = jnp.broadcast_to((jnp.arange(LATW) < LATW - 1)[:, None], (LATW, LONW))
    finished = apply_block(rolled, rolled_land, valid, w_qkv[1], w_out[1])
    return from_grid(jnp.roll(finished, (half_rows, half_cols), axis=(0, 1)))
```

```python
import functools

import jax
import jax.numpy as jnp
import numpy as np
from jax import lax
from jax.experimental import pallas as pl
from jax.experimental.pallas import tpu as pltpu
from jax.sharding import PartitionSpec as P

HD = 32
WH = 10
WW = 20
P_SIZE = WH * WW
ROWS = 4
PAD = 208
QR = 64
QT = 50
MESH = pl.DeviceIdType.MESH
SCALE = float(HD ** -0.5 * np.log2(np.e))
NEG = -1e30


def tables():
    token = np.arange(P_SIZE)
    i, j = token // WW, token % WW
    quad = (i // (WH // 2)) * 2 + j // (WW // 2)
    place = (i % (WH // 2)) * (WW // 2) + j % (WW // 2)
    split = np.zeros((4 * QR, PAD + 16), np.float32)
    split[quad * QR + place, token] = 1
    split[np.arange(4) * QR + QT, PAD + np.arange(4)] = 1
    join = np.zeros((PAD, 4 * QR), np.float32)
    join[token, quad * QR + place] = 1
    pick = np.zeros((PAD, 4 * QR), np.float32)
    pick[token, quad * QR + QT] = 1
    lane = np.zeros((PAD, 128), np.float32)
    lane[token, place] = 1
    member = np.zeros((16, PAD), np.float32)
    member[quad, token] = 1
    eye = np.eye(PAD, P_SIZE, dtype=np.float32)
    bf = jnp.bfloat16
    return (
        jnp.asarray(split, bf), jnp.asarray(join, bf), jnp.asarray(pick, bf),
        jnp.asarray(lane, bf), jnp.asarray(member, bf), jnp.asarray(eye),
    )


def mm(a, b):
    return jnp.dot(a, b, preferred_element_type=jnp.float32)


def mm_t(a, b):
    return lax.dot_general(a, b, (((1,), (1,)), ((), ())), preferred_element_type=jnp.float32)


def attend(x, land, wk, wqv, wo):
    bf = jnp.bfloat16
    width = wqv.shape[0] // 2
    half = width // 2
    centred = x - jnp.mean(x, axis=-1, keepdims=True)
    var = jnp.mean(centred * centred, axis=-1, keepdims=True)
    normed = (centred * lax.rsqrt(var + 1e-05)).astype(bf)
    qv = mm_t(wqv[...], normed)
    q = (qv[:width] * SCALE).astype(bf)
    v = qv[width:].astype(bf)
    mask = jnp.broadcast_to(land * NEG, (PAD, PAD))
    ones = jnp.ones((16, PAD), bf)
    outs = []
    for part in range(2):
        keys = mm(normed, wk[part]).astype(bf)
        for low in range(0, half, 128):
            high = min(low + 128, half)
            block = keys[:, low:high]
            for at in range(low, high, HD):
                row = part * half + at
                pieces = [q[row : row + HD]]
                if at > low:
                    pieces = [jnp.zeros((at - low, PAD), bf)] + pieces
                if at + HD < high:
                    pieces = pieces + [jnp.zeros((high - at - HD, PAD), bf)]
                query = jnp.concatenate(pieces, axis=0)
                scores = mm(block, query) + mask
                top = jnp.max(scores, axis=0, keepdims=True)
                powers = jnp.exp2(scores - top).astype(bf)
                value = jnp.concatenate([v[row : row + HD], ones], axis=0)
                mixed = mm(value, powers)
                outs.append((mixed[:HD] * (1.0 / mixed[HD : HD + 1])).astype(bf))
    blended = jnp.concatenate(outs, axis=0)
    return lax.dot_general(
        blended, wo[...], (((0,), (0,)), ((), ())), preferred_element_type=jnp.float32
    )


def kernel(
    tokens, land_rows, listed_row, w_qkv, w_out, split, join, pick, lane, member, eye,
    out,
    toks, wq_far, wo_far, wk_buf, wqv_buf, wo_buf, e, g, res,
    tok_sem, w_send, w_recv, col_send, col_recv, row_send, row_recv, dia_send, dia_recv,
    bcol_send, bcol_recv, brow_send, brow_recv, bdia_send, bdia_recv,
    o_send, o_recv, o_loc,
):
    bf = jnp.bfloat16
    wins = toks.shape[0]
    cols = wins // ROWS
    feat = toks.shape[2]
    half = w_qkv.shape[3]
    lon, lat, sub = lax.axis_index("lon"), lax.axis_index("lat"), lax.axis_index("sub")
    nlon, nlat, nsub = lax.axis_size("lon"), lax.axis_size("lat"), lax.axis_size("sub")
    spot = lon * nsub + sub
    after = lax.rem(spot + 1, nlon * nsub)
    before = lax.rem(spot + nlon * nsub - 1, nlon * nsub)
    up = lax.rem(lat + nlat - 1, nlat)
    down = lax.rem(lat + 1, nlat)
    mate = {"sub": 1 - sub}
    right = {"lon": after // nsub, "sub": lax.rem(after, nsub)}
    left = {"lon": before // nsub, "sub": lax.rem(before, nsub)}
    above, below = {"lat": up}, {"lat": down}
    left_up = dict(left, lat=up)
    right_down = dict(right, lat=down)
    base = sub * wins

    def load(c):
        return pltpu.make_async_copy(
            tokens.at[pl.ds(base + c * ROWS, ROWS)], toks.at[pl.ds(c * ROWS, ROWS)], tok_sem.at[c]
        )

    for c in range(cols):
        load(c).start()

    barrier = pltpu.get_barrier_semaphore()
    greeted = (mate, right, left, above, below, left_up, right_down)
    for other in greeted:
        pl.semaphore_signal(barrier, inc=1, device_id=other, device_id_type=MESH)
    pl.semaphore_wait(barrier, len(greeted))

    def send(src, dst, s, r, to):
        return pltpu.make_async_remote_copy(
            src_ref=src, dst_ref=dst, send_sem=s, recv_sem=r, device_id=to, device_id_type=MESH
        )

    weights = []
    for b in range(2):
        weights.append(send(w_qkv.at[b], wq_far.at[b], w_send.at[2 * b], w_recv.at[2 * b], mate))
        weights.append(
            send(w_out.at[b], wo_far.at[b], w_send.at[2 * b + 1], w_recv.at[2 * b + 1], mate)
        )
    for copy in weights:
        copy.start()

    def ready(b):
        for part, (wq, wo) in enumerate(((w_qkv, w_out), (wq_far, wo_far))):
            if part == 1:
                weights[2 * b].wait_recv()
                weights[2 * b + 1].wait_recv()
            low = part * half
            wqv_buf[low : low + half] = wq[b, 0].T
            wqv_buf[feat + low : feat + low + half] = wq[b, 2].T
            wk_buf[part] = wq[b, 1]
            wo_buf[low : low + half] = wo[b]

    def col_out(k):
        return send(
            e.at[0, pl.ds(0, ROWS), 2 * k], e.at[cols, pl.ds(0, ROWS), 2 * k],
            col_send.at[k], col_recv.at[k], left,
        )

    def row_out(c):
        return send(
            e.at[c, 0, pl.ds(0, 2)], e.at[c, ROWS, pl.ds(0, 2)],
            row_send.at[c], row_recv.at[c], above,
        )

    dia_out = send(e.at[0, 0, 0], e.at[cols, ROWS, 0], dia_send, dia_recv, left_up)

    pad_rows = jnp.zeros((PAD - P_SIZE, feat), jnp.float32)
    tail_land = (lax.broadcasted_iota(jnp.int32, (PAD, 1), 0) >= P_SIZE).astype(jnp.float32)
    ready(0)

    def one(c, r):
        w = c * ROWS + r
        x = jnp.concatenate([toks[w].astype(jnp.float32), pad_rows], axis=0)
        row = land_rows[base + w].astype(jnp.float32)
        land = jnp.sum(eye[...] * row, axis=1, keepdims=True) + tail_land
        mine = spot * wins + w
        listed = jnp.max(
            jnp.where(listed_row[...] == mine, 1.0, 0.0), axis=1, keepdims=True
        )
        update = attend(x, land, wk_buf, wqv_buf, wo_buf)
        first = (x + update * (listed * (1.0 - land))).astype(bf)
        wide = jnp.concatenate([row, jnp.zeros((1, PAD - P_SIZE), jnp.float32)], axis=1)
        quads_land = mm((member[...].astype(jnp.float32) * wide).astype(bf), lane[...]).astype(bf)
        quads_land = jnp.concatenate([quads_land, jnp.zeros((16, feat - 128), bf)], axis=1)
        quads = mm(split[...], jnp.concatenate([first, quads_land], axis=0)).astype(bf)
        e[c, r] = quads.reshape(4, QR, feat)

    def first_column(c, carry):
        load(c).wait()

        def step(r, inner):
            one(c, r)

            @pl.when(r == 0)
            def _():
                row_out(c).start()

            return inner

        lax.fori_loop(0, ROWS, step, 0)

        @pl.when(c == 0)
        def _():
            col_out(0).start()
            col_out(1).start()
            dia_out.start()

        return carry

    lax.fori_loop(0, cols, first_column, 0)
    ready(1)
    col_out(0).wait_recv()
    col_out(1).wait_recv()
    dia_out.wait_recv()
    for c in range(cols):
        row_out(c).wait_recv()

    def bcol_out(k):
        return send(
            g.at[cols, pl.ds(1, ROWS), 2 * k + 1], g.at[0, pl.ds(1, ROWS), 2 * k + 1],
            bcol_send.at[k], bcol_recv.at[k], right,
        )

    def brow_out(c):
        return send(
            g.at[c + 1, ROWS, pl.ds(2, 2)], g.at[c + 1, 0, pl.ds(2, 2)],
            brow_send.at[c], brow_recv.at[c], below,
        )

    bdia_out = send(g.at[cols, ROWS, 3], g.at[0, 0, 3], bdia_send, bdia_recv, right_down)

    def two(c, r):
        quads = jnp.concatenate(
            [e[c, r, 3], e[c + 1, r, 2], e[c, r + 1, 1], e[c + 1, r + 1, 0]], axis=0
        )
        x = mm(join[...], quads)
        rows = mm(pick[...], quads[:, :128])
        land = jnp.sum(rows * lane[...].astype(jnp.float32), axis=1, keepdims=True) + tail_land
        edge = jnp.logical_and(lat == nlat - 1, r == ROWS - 1)
        inside = 1.0 - edge.astype(jnp.float32)
        update = attend(x, land, wk_buf, wqv_buf, wo_buf)
        finished = (x + update * ((1.0 - land) * inside)).astype(bf)
        g[c + 1, r + 1] = mm(split[:, :PAD], finished).astype(bf).reshape(4, QR, feat)

    def mate_out(c):
        return send(
            res.at[pl.ds(c * ROWS, ROWS)], out.at[pl.ds(base + c * ROWS, ROWS)],
            o_send.at[c], o_recv.at[c], mate,
        )

    def own_out(c):
        return pltpu.make_async_copy(
            res.at[pl.ds(c * ROWS, ROWS)], out.at[pl.ds(base + c * ROWS, ROWS)], o_loc.at[c]
        )

    def restore(c):
        def step(r, inner):
            quads = jnp.concatenate(
                [g[c, r, 3], g[c + 1, r, 2], g[c, r + 1, 1], g[c + 1, r + 1, 0]], axis=0
            )
            res[c * ROWS + r] = mm(join[...], quads)[:P_SIZE].astype(bf)
            return inner

        lax.fori_loop(0, ROWS, step, 0)
        mate_out(c).start()
        own_out(c).start()

    def second_column(t, carry):
        c = cols - 1 - t

        def step(u, inner):
            two(c, ROWS - 1 - u)

            @pl.when(u == 0)
            def _():
                brow_out(c).start()

            return inner

        lax.fori_loop(0, ROWS, step, 0)

        @pl.when(t == 0)
        def _():
            bcol_out(0).start()
            bcol_out(1).start()
            bdia_out.start()
            brow_out(cols - 1).wait_recv()

        @pl.when(t > 0)
        def _():
            brow_out(c).wait_recv()
            restore(c + 1)

        return carry

    lax.fori_loop(0, cols, second_column, 0)
    bcol_out(0).wait_recv()
    bcol_out(1).wait_recv()
    bdia_out.wait_recv()
    restore(0)

    for copy in weights + [dia_out, bdia_out] + [f(k) for f in (col_out, bcol_out) for k in (0, 1)]:
        copy.wait_send()
    for c in range(cols):
        row_out(c).wait_send()
        brow_out(c).wait_send()
        own_out(c).wait()
        mate_out(c).wait_send()
        far = (1 - sub) * wins + c * ROWS
        send(
            res.at[pl.ds(c * ROWS, ROWS)], out.at[pl.ds(far, ROWS)],
            o_send.at[c], o_recv.at[c], mate,
        ).wait_recv()


def shards(tokens, land_bits, ocean_list, w_qkv, w_out):
    bf = jnp.bfloat16
    count, size, feat = tokens.shape
    wins = count // lax.axis_size("sub")
    cols = wins // ROWS
    half = w_qkv.shape[3]
    vmem = pl.BlockSpec(memory_space=pltpu.VMEM)
    anywhere = pl.BlockSpec(memory_space=pl.ANY)
    dma = pltpu.SemaphoreType.DMA
    return pl.pallas_call(
        kernel,
        out_shape=jax.ShapeDtypeStruct(tokens.shape, bf),
        in_specs=[anywhere] + [vmem] * 10,
        out_specs=anywhere,
        scratch_shapes=[
            pltpu.VMEM((wins, size, feat), bf),
            pltpu.VMEM(w_qkv.shape, bf),
            pltpu.VMEM(w_out.shape, bf),
            pltpu.VMEM((2, feat, half), bf),
            pltpu.VMEM((2 * feat, feat), bf),
            pltpu.VMEM((feat, feat), bf),
            pltpu.VMEM((cols + 1, ROWS + 1, 4, QR, feat), bf),
            pltpu.VMEM((cols + 1, ROWS + 1, 4, QR, feat), bf),
            pltpu.VMEM((wins, size, feat), bf),
            dma((cols,)), dma((4,)), dma((4,)),
            dma((2,)), dma((2,)), dma((cols,)), dma((cols,)), dma(()), dma(()),
            dma((2,)), dma((2,)), dma((cols,)), dma((cols,)), dma(()), dma(()),
            dma((cols,)), dma((cols,)), dma((cols,)),
        ],
        compiler_params=pltpu.CompilerParams(
            collective_id=0, has_side_effects=True, vmem_limit_bytes=48 * 1024 * 1024
        ),
    )(tokens, land_bits.reshape(count, 1, size), ocean_list, w_qkv, w_out, *tables())


def solution(mesh):
    placed = (
        P(("groups", "lat", "lon"), None, None),
        P(("groups", "lat", "lon"), None),
        P(("groups", "lat"), None),
        P(None, None, None, "sub"),
        P(None, "sub", None),
    )
    return jax.shard_map(
        shards,
        mesh=mesh,
        in_specs=placed,
        out_specs=P(("groups", "lat", "lon"), None, None),
        check_vma=False,
    )
```

```python
import functools

import jax
import jax.numpy as jnp
import numpy as np
from jax import lax
from jax.experimental import pallas as pl
from jax.experimental.pallas import tpu as pltpu
from jax.sharding import PartitionSpec as P

HD = 32
WH = 10
WW = 20
P_SIZE = WH * WW
ROWS = 4
PAD = 208
QR = 64
QT = 50
MESH = pl.DeviceIdType.MESH
SCALE = float(HD ** -0.5 * np.log2(np.e))
NEG = -1e30


def tables():
    token = np.arange(P_SIZE)
    i, j = token // WW, token % WW
    quad = (i // (WH // 2)) * 2 + j // (WW // 2)
    place = (i % (WH // 2)) * (WW // 2) + j % (WW // 2)
    split = np.zeros((4 * QR, PAD + 16), np.float32)
    split[quad * QR + place, token] = 1
    split[np.arange(4) * QR + QT, PAD + np.arange(4)] = 1
    join = np.zeros((PAD, 4 * QR), np.float32)
    join[token, quad * QR + place] = 1
    pick = np.zeros((PAD, 4 * QR), np.float32)
    pick[token, quad * QR + QT] = 1
    gather = np.zeros((16, 4 * QR), np.float32)
    gather[np.arange(4), np.arange(4) * QR + QT] = 1
    lane = np.zeros((PAD, 128), np.float32)
    lane[token, place] = 1
    member = np.zeros((16, PAD), np.float32)
    member[quad, token] = 1
    eye = np.eye(PAD, P_SIZE, dtype=np.float32)
    bf = jnp.bfloat16
    return (
        jnp.asarray(split, bf), jnp.asarray(join, bf), jnp.asarray(pick, bf),
        jnp.asarray(gather, bf), jnp.asarray(lane, bf), jnp.asarray(member, bf), jnp.asarray(eye),
    )


def mm(a, b):
    return jnp.dot(a, b, preferred_element_type=jnp.float32)


def mm_t(a, b):
    return lax.dot_general(a, b, (((1,), (1,)), ((), ())), preferred_element_type=jnp.float32)


def attend(x, land, w_all, wo):
    bf = jnp.bfloat16
    width = wo.shape[0]
    centred = x - jnp.mean(x, axis=-1, keepdims=True)
    var = jnp.mean(centred * centred, axis=-1, keepdims=True)
    normed = (centred * lax.rsqrt(var + 1e-05)).astype(bf)
    qkv = mm(normed, w_all[...])
    q = (qkv[:, :width] * SCALE).astype(bf)
    k = qkv[:, width : 2 * width].astype(bf)
    v = qkv[:, 2 * width :].astype(bf)
    mask = jnp.broadcast_to(land * NEG, (PAD, PAD))
    head = lax.broadcasted_iota(jnp.int32, (1, 128), 1) // HD
    ones = jnp.ones((PAD, 128), bf)
    outs = []
    for low in range(0, width, 128):
        query, key, value = (t[:, low : low + 128] for t in (q, k, v))
        total = None
        for h in range(128 // HD):
            own = jnp.broadcast_to(jnp.where(head == h, 1.0, 0.0).astype(bf), (PAD, 128))
            scores = mm_t(query * own, key) + mask
            top = jnp.max(scores, axis=1, keepdims=True)
            powers = jnp.exp2(scores - top).astype(bf)
            mixed = mm(powers, jnp.concatenate([value * own, ones], axis=1))
            mixed = mixed[:, :128] * (1.0 / mixed[:, 128:])
            total = mixed if total is None else total + mixed
        outs.append(total.astype(bf))
    return mm(jnp.concatenate(outs, axis=1), wo[...])


def kernel(
    tokens, land_rows, listed_row, w_qkv, w_out, split, join, pick, gather, lane, member, eye,
    out,
    toks, wq_far, wo_far, w_buf, wo_buf, e, g, res,
    tok_sem, w_send, w_recv, col_send, col_recv, row_send, row_recv, dia_send, dia_recv,
    bcol_send, bcol_recv, brow_send, brow_recv, bdia_send, bdia_recv,
    o_send, o_recv, o_loc,
):
    bf = jnp.bfloat16
    wins = toks.shape[0]
    cols = wins // ROWS
    feat = toks.shape[2]
    half = w_qkv.shape[3]
    lon, lat, sub = lax.axis_index("lon"), lax.axis_index("lat"), lax.axis_index("sub")
    nlon, nlat, nsub = lax.axis_size("lon"), lax.axis_size("lat"), lax.axis_size("sub")
    spot = lon * nsub + sub
    after = lax.rem(spot + 1, nlon * nsub)
    before = lax.rem(spot + nlon * nsub - 1, nlon * nsub)
    up = lax.rem(lat + nlat - 1, nlat)
    down = lax.rem(lat + 1, nlat)
    mate = {"sub": 1 - sub}
    right = {"lon": after // nsub, "sub": lax.rem(after, nsub)}
    left = {"lon": before // nsub, "sub": lax.rem(before, nsub)}
    above, below = {"lat": up}, {"lat": down}
    left_up = dict(left, lat=up)
    right_down = dict(right, lat=down)
    base = sub * wins

    def load(c):
        return pltpu.make_async_copy(
            tokens.at[pl.ds(base + c * ROWS, ROWS)], toks.at[pl.ds(c * ROWS, ROWS)], tok_sem.at[c]
        )

    for c in range(cols):
        load(c).start()

    barrier = pltpu.get_barrier_semaphore()
    greeted = (mate, right, left, above, below, left_up, right_down)
    for other in greeted:
        pl.semaphore_signal(barrier, inc=1, device_id=other, device_id_type=MESH)
    pl.semaphore_wait(barrier, len(greeted))

    def send(src, dst, s, r, to):
        return pltpu.make_async_remote_copy(
            src_ref=src, dst_ref=dst, send_sem=s, recv_sem=r, device_id=to, device_id_type=MESH
        )

    weights = []
    for b in range(2):
        weights.append(send(w_qkv.at[b], wq_far.at[b], w_send.at[2 * b], w_recv.at[2 * b], mate))
        weights.append(
            send(w_out.at[b], wo_far.at[b], w_send.at[2 * b + 1], w_recv.at[2 * b + 1], mate)
        )
    for copy in weights:
        copy.start()

    def ready(b):
        for part, (wq, wo) in enumerate(((w_qkv, w_out), (wq_far, wo_far))):
            if part == 1:
                weights[2 * b].wait_recv()
                weights[2 * b + 1].wait_recv()
            low = part * half
            wo_buf[low : low + half] = wo[b]
        for kind in range(3):
            w_buf[:, kind * feat : (kind + 1) * feat] = jnp.concatenate(
                [w_qkv[b, kind], wq_far[b, kind]], axis=1
            )

    def col_out(k):
        return send(
            e.at[0, pl.ds(0, ROWS), 2 * k], e.at[cols, pl.ds(0, ROWS), 2 * k],
            col_send.at[k], col_recv.at[k], left,
        )

    def row_out(c):
        return send(
            e.at[c, 0, pl.ds(0, 2)], e.at[c, ROWS, pl.ds(0, 2)],
            row_send.at[c], row_recv.at[c], above,
        )

    dia_out = send(e.at[0, 0, 0], e.at[cols, ROWS, 0], dia_send, dia_recv, left_up)

    pad_rows = jnp.zeros((PAD - P_SIZE, feat), jnp.float32)
    tail_land = (lax.broadcasted_iota(jnp.int32, (PAD, 1), 0) >= P_SIZE).astype(jnp.float32)
    tail_row = (lax.broadcasted_iota(jnp.int32, (1, PAD), 1) >= P_SIZE).astype(jnp.float32)
    ready(0)

    def one(c, r):
        w = c * ROWS + r
        x = jnp.concatenate([toks[w].astype(jnp.float32), pad_rows], axis=0)
        row = land_rows[base + w].astype(jnp.float32)
        land = jnp.sum(eye[...] * row, axis=1, keepdims=True) + tail_land
        wide = jnp.concatenate([row, jnp.zeros((1, PAD - P_SIZE), jnp.float32)], axis=1)
        land_row = wide + tail_row
        mine = spot * wins + w
        listed = jnp.max(
            jnp.where(listed_row[...] == mine, 1.0, 0.0), axis=1, keepdims=True
        )
        update = attend(x, land_row, w_buf, wo_buf)
        first = (x + update * (listed * (1.0 - land))).astype(bf)
        quads_land = mm((member[...].astype(jnp.float32) * wide).astype(bf), lane[...]).astype(bf)
        quads_land = jnp.concatenate([quads_land, jnp.zeros((16, feat - 128), bf)], axis=1)
        quads = mm(split[...], jnp.concatenate([first, quads_land], axis=0)).astype(bf)
        e[c, r] = quads.reshape(4, QR, feat)

    def first_column(c, carry):
        load(c).wait()

        def step(pair, inner):
            for r in range(2):
                one(c, 2 * pair + r)

            @pl.when(pair == 0)
            def _():
                row_out(c).start()

            return inner

        lax.fori_loop(0, ROWS // 2, step, 0)

        @pl.when(c == 0)
        def _():
            col_out(0).start()
            col_out(1).start()
            dia_out.start()

        return carry

    lax.fori_loop(0, cols, first_column, 0)
    ready(1)
    col_out(0).wait_recv()
    col_out(1).wait_recv()
    dia_out.wait_recv()
    for c in range(cols):
        row_out(c).wait_recv()

    def bcol_out(k):
        return send(
            g.at[cols, pl.ds(1, ROWS), 2 * k + 1], g.at[0, pl.ds(1, ROWS), 2 * k + 1],
            bcol_send.at[k], bcol_recv.at[k], right,
        )

    def brow_out(c):
        return send(
            g.at[c + 1, ROWS, pl.ds(2, 2)], g.at[c + 1, 0, pl.ds(2, 2)],
            brow_send.at[c], brow_recv.at[c], below,
        )

    bdia_out = send(g.at[cols, ROWS, 3], g.at[0, 0, 3], bdia_send, bdia_recv, right_down)

    def two(c, r):
        quads = jnp.concatenate(
            [e[c, r, 3], e[c + 1, r, 2], e[c, r + 1, 1], e[c + 1, r + 1, 0]], axis=0
        )
        x = mm(join[...], quads)
        rows = mm(pick[...], quads[:, :128])
        land = jnp.sum(rows * lane[...].astype(jnp.float32), axis=1, keepdims=True) + tail_land
        spread = mm_t(mm(gather[...], quads[:, :128]).astype(bf), lane[...])
        land_row = jnp.sum(spread * member[...].astype(jnp.float32), axis=0, keepdims=True)
        land_row = land_row + tail_row
        edge = jnp.logical_and(lat == nlat - 1, r == ROWS - 1)
        inside = 1.0 - edge.astype(jnp.float32)
        update = attend(x, land_row, w_buf, wo_buf)
        finished = (x + update * ((1.0 - land) * inside)).astype(bf)
        g[c + 1, r + 1] = mm(split[:, :PAD], finished).astype(bf).reshape(4, QR, feat)

    def mate_out(c):
        return send(
            res.at[pl.ds(c * ROWS, ROWS)], out.at[pl.ds(base + c * ROWS, ROWS)],
            o_send.at[c], o_recv.at[c], mate,
        )

    def own_out(c):
        return pltpu.make_async_copy(
            res.at[pl.ds(c * ROWS, ROWS)], out.at[pl.ds(base + c * ROWS, ROWS)], o_loc.at[c]
        )

    def restore(c):
        def step(r, inner):
            quads = jnp.concatenate(
                [g[c, r, 3], g[c + 1, r, 2], g[c, r + 1, 1], g[c + 1, r + 1, 0]], axis=0
            )
            res[c * ROWS + r] = mm(join[...], quads)[:P_SIZE].astype(bf)
            return inner

        lax.fori_loop(0, ROWS, step, 0)
        mate_out(c).start()
        own_out(c).start()

    def second_column(t, carry):
        c = cols - 1 - t

        def step(pair, inner):
            for u in range(2):
                two(c, ROWS - 1 - u - 2 * pair)

            @pl.when(pair == 0)
            def _():
                brow_out(c).start()

            return inner

        lax.fori_loop(0, ROWS // 2, step, 0)

        @pl.when(t == 0)
        def _():
            bcol_out(0).start()
            bcol_out(1).start()
            bdia_out.start()
            brow_out(cols - 1).wait_recv()

        @pl.when(t > 0)
        def _():
            brow_out(c).wait_recv()
            restore(c + 1)

        return carry

    lax.fori_loop(0, cols, second_column, 0)
    bcol_out(0).wait_recv()
    bcol_out(1).wait_recv()
    bdia_out.wait_recv()
    restore(0)

    for copy in weights + [dia_out, bdia_out] + [f(k) for f in (col_out, bcol_out) for k in (0, 1)]:
        copy.wait_send()
    for c in range(cols):
        row_out(c).wait_send()
        brow_out(c).wait_send()
        own_out(c).wait()
        mate_out(c).wait_send()
        far = (1 - sub) * wins + c * ROWS
        send(
            res.at[pl.ds(c * ROWS, ROWS)], out.at[pl.ds(far, ROWS)],
            o_send.at[c], o_recv.at[c], mate,
        ).wait_recv()


def shards(tokens, land_bits, ocean_list, w_qkv, w_out):
    bf = jnp.bfloat16
    count, size, feat = tokens.shape
    wins = count // lax.axis_size("sub")
    cols = wins // ROWS
    vmem = pl.BlockSpec(memory_space=pltpu.VMEM)
    anywhere = pl.BlockSpec(memory_space=pl.ANY)
    dma = pltpu.SemaphoreType.DMA
    return pl.pallas_call(
        kernel,
        out_shape=jax.ShapeDtypeStruct(tokens.shape, bf),
        in_specs=[anywhere] + [vmem] * 11,
        out_specs=anywhere,
        scratch_shapes=[
            pltpu.VMEM((wins, size, feat), bf),
            pltpu.VMEM(w_qkv.shape, bf),
            pltpu.VMEM(w_out.shape, bf),
            pltpu.VMEM((feat, 3 * feat), bf),
            pltpu.VMEM((feat, feat), bf),
            pltpu.VMEM((cols + 1, ROWS + 1, 4, QR, feat), bf),
            pltpu.VMEM((cols + 1, ROWS + 1, 4, QR, feat), bf),
            pltpu.VMEM((wins, size, feat), bf),
            dma((cols,)), dma((4,)), dma((4,)),
            dma((2,)), dma((2,)), dma((cols,)), dma((cols,)), dma(()), dma(()),
            dma((2,)), dma((2,)), dma((cols,)), dma((cols,)), dma(()), dma(()),
            dma((cols,)), dma((cols,)), dma((cols,)),
        ],
        compiler_params=pltpu.CompilerParams(
            collective_id=0, has_side_effects=True, vmem_limit_bytes=48 * 1024 * 1024
        ),
    )(tokens, land_bits.reshape(count, 1, size), ocean_list, w_qkv, w_out, *tables())


def solution(mesh):
    placed = (
        P(("groups", "lat", "lon"), None, None),
        P(("groups", "lat", "lon"), None),
        P(("groups", "lat"), None),
        P(None, None, None, "sub"),
        P(None, "sub", None),
    )
    return jax.shard_map(
        shards,
        mesh=mesh,
        in_specs=placed,
        out_specs=P(("groups", "lat", "lon"), None, None),
        check_vma=False,
    )
```

```python
import jax
import jax.numpy as jnp
import numpy as np
from jax import lax
from jax.experimental import pallas as pl
from jax.experimental.pallas import tpu as pltpu
from jax.sharding import PartitionSpec as P

HD = 32
WH = 10
WW = 20
P_SIZE = WH * WW
ROWS = 4
PAD = 208
QR = 64
QT = 50
MESH = pl.DeviceIdType.MESH
SCALE = float(HD ** -0.5 * np.log2(np.e))
NEG = -1e30


def tables():
    token = np.arange(P_SIZE)
    i, j = token // WW, token % WW
    quad = (i // (WH // 2)) * 2 + j // (WW // 2)
    place = (i % (WH // 2)) * (WW // 2) + j % (WW // 2)
    split = np.zeros((4 * QR, PAD + 16), np.float32)
    split[quad * QR + place, token] = 1
    split[np.arange(4) * QR + QT, PAD + np.arange(4)] = 1
    join = np.zeros((PAD, 4 * QR), np.float32)
    join[token, quad * QR + place] = 1
    pick = np.zeros((PAD, 4 * QR), np.float32)
    pick[token, quad * QR + QT] = 1
    gather = np.zeros((16, 4 * QR), np.float32)
    gather[np.arange(4), np.arange(4) * QR + QT] = 1
    lane = np.zeros((PAD, 128), np.float32)
    lane[token, place] = 1
    member = np.zeros((16, PAD), np.float32)
    member[quad, token] = 1
    eye = np.eye(PAD, P_SIZE, dtype=np.float32)
    parts = [np.pad(t, ((0, 0), (0, 256 - t.shape[1]))) for t in (split, join, pick, gather, lane, member, eye)]
    return jnp.asarray(np.concatenate(parts), jnp.bfloat16)


SPANS = (256, PAD, PAD, 16, PAD, 16, PAD)


def mm(a, b):
    return jnp.dot(a, b, preferred_element_type=jnp.float32)


def mm_t(a, b):
    return lax.dot_general(a, b, (((1,), (1,)), ((), ())), preferred_element_type=jnp.float32)


def attend(x, land, w_all, wo):
    bf = jnp.bfloat16
    width = wo.shape[0]
    centred = x - jnp.mean(x, axis=-1, keepdims=True)
    var = jnp.mean(centred * centred, axis=-1, keepdims=True)
    normed = (centred * lax.rsqrt(var + 1e-05)).astype(bf)
    qkv = mm(normed, w_all[...])
    q = (qkv[:, :width] * SCALE).astype(bf)
    k = qkv[:, width : 2 * width].astype(bf)
    v = qkv[:, 2 * width :].astype(bf)
    mask = jnp.broadcast_to(land * NEG, (PAD, PAD))
    head = lax.broadcasted_iota(jnp.int32, (1, 128), 1) // HD
    ones = jnp.ones((PAD, 128), bf)
    outs = []
    for low in range(0, width, 128):
        query, key, value = (t[:, low : low + 128] for t in (q, k, v))
        total = None
        for h in range(128 // HD):
            own = jnp.broadcast_to(jnp.where(head == h, 1.0, 0.0).astype(bf), (PAD, 128))
            scores = mm_t(query * own, key) + mask
            top = jnp.max(scores, axis=1, keepdims=True)
            powers = jnp.exp2(scores - top).astype(bf)
            mixed = mm(powers, jnp.concatenate([value * own, ones], axis=1))
            mixed = mixed[:, :128] * (1.0 / mixed[:, 128:])
            total = mixed if total is None else total + mixed
        outs.append(total.astype(bf))
    return mm(jnp.concatenate(outs, axis=1), wo[...])


def kernel(
    tokens, land_rows, listed_row, w_qkv, w_out, table,
    out,
    toks, wq_far, wo_far, w_buf, wo_buf, e, g, res,
    tok_sem, w_send, w_recv, col_send, col_recv, row_send, row_recv, dia_send, dia_recv,
    bcol_send, bcol_recv, brow_send, brow_recv, bdia_send, bdia_recv,
    o_send, o_recv, o_loc,
):
    bf = jnp.bfloat16
    views, start = [], 0
    for tall in SPANS:
        views.append(table.at[pl.ds(start, tall)])
        start += tall
    split, join, pick, gather, lane, member, eye = views
    wins = toks.shape[0]
    cols = wins // ROWS
    feat = toks.shape[2]
    half = w_qkv.shape[3]
    lon, lat, sub = lax.axis_index("lon"), lax.axis_index("lat"), lax.axis_index("sub")
    nlon, nlat, nsub = lax.axis_size("lon"), lax.axis_size("lat"), lax.axis_size("sub")
    spot = lon * nsub + sub
    after = lax.rem(spot + 1, nlon * nsub)
    before = lax.rem(spot + nlon * nsub - 1, nlon * nsub)
    up = lax.rem(lat + nlat - 1, nlat)
    down = lax.rem(lat + 1, nlat)
    mate = {"sub": 1 - sub}
    right = {"lon": after // nsub, "sub": lax.rem(after, nsub)}
    left = {"lon": before // nsub, "sub": lax.rem(before, nsub)}
    above, below = {"lat": up}, {"lat": down}
    left_up = dict(left, lat=up)
    right_down = dict(right, lat=down)
    base = sub * wins

    def load(c):
        return pltpu.make_async_copy(
            tokens.at[pl.ds(base + c * ROWS, ROWS)], toks.at[pl.ds(c * ROWS, ROWS)], tok_sem.at[c]
        )

    for c in range(cols):
        load(c).start()

    barrier = pltpu.get_barrier_semaphore()
    greeted = (mate, right, left, above, below, left_up, right_down)
    for other in greeted:
        pl.semaphore_signal(barrier, inc=1, device_id=other, device_id_type=MESH)
    pl.semaphore_wait(barrier, len(greeted))

    def send(src, dst, s, r, to):
        return pltpu.make_async_remote_copy(
            src_ref=src, dst_ref=dst, send_sem=s, recv_sem=r, device_id=to, device_id_type=MESH
        )

    weights = []
    for b in range(2):
        weights.append(send(w_qkv.at[b], wq_far.at[b], w_send.at[2 * b], w_recv.at[2 * b], mate))
        weights.append(
            send(w_out.at[b], wo_far.at[b], w_send.at[2 * b + 1], w_recv.at[2 * b + 1], mate)
        )
    for copy in weights:
        copy.start()

    def ready(b):
        for part, (wq, wo) in enumerate(((w_qkv, w_out), (wq_far, wo_far))):
            if part == 1:
                weights[2 * b].wait_recv()
                weights[2 * b + 1].wait_recv()
            low = part * half
            wo_buf[low : low + half] = wo[b]
        for kind in range(3):
            w_buf[:, kind * feat : (kind + 1) * feat] = jnp.concatenate(
                [w_qkv[b, kind], wq_far[b, kind]], axis=1
            )

    def col_out(k):
        return send(
            e.at[0, pl.ds(0, ROWS), 2 * k], e.at[cols, pl.ds(0, ROWS), 2 * k],
            col_send.at[k], col_recv.at[k], left,
        )

    def row_out(c):
        return send(
            e.at[c, 0, pl.ds(0, 2)], e.at[c, ROWS, pl.ds(0, 2)],
            row_send.at[c], row_recv.at[c], above,
        )

    dia_out = send(e.at[0, 0, 0], e.at[cols, ROWS, 0], dia_send, dia_recv, left_up)

    pad_rows = jnp.zeros((PAD - P_SIZE, feat), jnp.float32)
    tail_land = (lax.broadcasted_iota(jnp.int32, (PAD, 1), 0) >= P_SIZE).astype(jnp.float32)
    tail_row = (lax.broadcasted_iota(jnp.int32, (1, PAD), 1) >= P_SIZE).astype(jnp.float32)
    ready(0)

    def one(c, r):
        w = c * ROWS + r
        x = jnp.concatenate([toks[w].astype(jnp.float32), pad_rows], axis=0)
        row = land_rows[base + w].astype(jnp.float32)
        land = jnp.sum(eye[:, :P_SIZE].astype(jnp.float32) * row, axis=1, keepdims=True) + tail_land
        wide = jnp.concatenate([row, jnp.zeros((1, PAD - P_SIZE), jnp.float32)], axis=1)
        land_row = wide + tail_row
        mine = spot * wins + w
        listed = jnp.max(
            jnp.where(listed_row[...] == mine, 1.0, 0.0), axis=1, keepdims=True
        )
        update = attend(x, land_row, w_buf, wo_buf)
        first = (x + update * (listed * (1.0 - land))).astype(bf)
        quads_land = mm((member[:, :PAD].astype(jnp.float32) * wide).astype(bf), lane[:, :128]).astype(bf)
        quads_land = jnp.concatenate([quads_land, jnp.zeros((16, feat - 128), bf)], axis=1)
        quads = mm(split[:, : PAD + 16], jnp.concatenate([first, quads_land], axis=0)).astype(bf)
        e[c, r] = quads.reshape(4, QR, feat)

    def first_column(c, carry):
        load(c).wait()

        def step(pair, inner):
            for r in range(2):
                one(c, 2 * pair + r)

            @pl.when(pair == 0)
            def _():
                row_out(c).start()

            return inner

        lax.fori_loop(0, ROWS // 2, step, 0)

        @pl.when(c == 0)
        def _():
            col_out(0).start()
            col_out(1).start()
            dia_out.start()

        return carry

    lax.fori_loop(0, cols, first_column, 0)
    ready(1)
    col_out(0).wait_recv()
    col_out(1).wait_recv()
    dia_out.wait_recv()
    for c in range(cols):
        row_out(c).wait_recv()

    def bcol_out(k):
        return send(
            g.at[cols, pl.ds(1, ROWS), 2 * k + 1], g.at[0, pl.ds(1, ROWS), 2 * k + 1],
            bcol_send.at[k], bcol_recv.at[k], right,
        )

    def brow_out(c):
        return send(
            g.at[c + 1, ROWS, pl.ds(2, 2)], g.at[c + 1, 0, pl.ds(2, 2)],
            brow_send.at[c], brow_recv.at[c], below,
        )

    bdia_out = send(g.at[cols, ROWS, 3], g.at[0, 0, 3], bdia_send, bdia_recv, right_down)

    def two(c, r):
        quads = jnp.concatenate(
            [e[c, r, 3], e[c + 1, r, 2], e[c, r + 1, 1], e[c + 1, r + 1, 0]], axis=0
        )
        x = mm(join[...], quads)
        rows = mm(pick[...], quads[:, :128])
        land = jnp.sum(rows * lane[:, :128].astype(jnp.float32), axis=1, keepdims=True) + tail_land
        spread = mm_t(mm(gather[...], quads[:, :128]).astype(bf), lane[:, :128])
        land_row = jnp.sum(spread * member[:, :PAD].astype(jnp.float32), axis=0, keepdims=True)
        land_row = land_row + tail_row
        edge = jnp.logical_and(lat == nlat - 1, r == ROWS - 1)
        inside = 1.0 - edge.astype(jnp.float32)
        update = attend(x, land_row, w_buf, wo_buf)
        finished = (x + update * ((1.0 - land) * inside)).astype(bf)
        g[c + 1, r + 1] = mm(split[:, :PAD], finished).astype(bf).reshape(4, QR, feat)

    def mate_out(c):
        return send(
            res.at[pl.ds(c * ROWS, ROWS)], out.at[pl.ds(base + c * ROWS, ROWS)],
            o_send.at[c], o_recv.at[c], mate,
        )

    def own_out(c):
        return pltpu.make_async_copy(
            res.at[pl.ds(c * ROWS, ROWS)], out.at[pl.ds(base + c * ROWS, ROWS)], o_loc.at[c]
        )

    def restore(c):
        def step(r, inner):
            quads = jnp.concatenate(
                [g[c, r, 3], g[c + 1, r, 2], g[c, r + 1, 1], g[c + 1, r + 1, 0]], axis=0
            )
            res[c * ROWS + r] = mm(join[...], quads)[:P_SIZE].astype(bf)
            return inner

        lax.fori_loop(0, ROWS, step, 0)
        mate_out(c).start()
        own_out(c).start()

    def second_column(t, carry):
        c = cols - 1 - t

        def step(pair, inner):
            for u in range(2):
                two(c, ROWS - 1 - u - 2 * pair)

            @pl.when(pair == 0)
            def _():
                brow_out(c).start()

            return inner

        lax.fori_loop(0, ROWS // 2, step, 0)

        @pl.when(t == 0)
        def _():
            bcol_out(0).start()
            bcol_out(1).start()
            bdia_out.start()
            brow_out(cols - 1).wait_recv()

        @pl.when(t > 0)
        def _():
            brow_out(c).wait_recv()
            restore(c + 1)

        return carry

    lax.fori_loop(0, cols, second_column, 0)
    bcol_out(0).wait_recv()
    bcol_out(1).wait_recv()
    bdia_out.wait_recv()
    restore(0)

    for copy in weights + [dia_out, bdia_out] + [f(k) for f in (col_out, bcol_out) for k in (0, 1)]:
        copy.wait_send()
    for c in range(cols):
        row_out(c).wait_send()
        brow_out(c).wait_send()
        own_out(c).wait()
        mate_out(c).wait_send()
        far = (1 - sub) * wins + c * ROWS
        send(
            res.at[pl.ds(c * ROWS, ROWS)], out.at[pl.ds(far, ROWS)],
            o_send.at[c], o_recv.at[c], mate,
        ).wait_recv()


def shards(tokens, land_bits, ocean_list, w_qkv, w_out):
    bf = jnp.bfloat16
    count, size, feat = tokens.shape
    wins = count // lax.axis_size("sub")
    cols = wins // ROWS
    vmem = pl.BlockSpec(memory_space=pltpu.VMEM)
    anywhere = pl.BlockSpec(memory_space=pl.ANY)
    dma = pltpu.SemaphoreType.DMA
    return pl.pallas_call(
        kernel,
        out_shape=jax.ShapeDtypeStruct(tokens.shape, bf),
        in_specs=[anywhere] + [vmem] * 5,
        out_specs=anywhere,
        scratch_shapes=[
            pltpu.VMEM((wins, size, feat), bf),
            pltpu.VMEM(w_qkv.shape, bf),
            pltpu.VMEM(w_out.shape, bf),
            pltpu.VMEM((feat, 3 * feat), bf),
            pltpu.VMEM((feat, feat), bf),
            pltpu.VMEM((cols + 1, ROWS + 1, 4, QR, feat), bf),
            pltpu.VMEM((cols + 1, ROWS + 1, 4, QR, feat), bf),
            pltpu.VMEM((wins, size, feat), bf),
            dma((cols,)), dma((4,)), dma((4,)),
            dma((2,)), dma((2,)), dma((cols,)), dma((cols,)), dma(()), dma(()),
            dma((2,)), dma((2,)), dma((cols,)), dma((cols,)), dma(()), dma(()),
            dma((cols,)), dma((cols,)), dma((cols,)),
        ],
        compiler_params=pltpu.CompilerParams(
            collective_id=0, has_side_effects=True, vmem_limit_bytes=48 * 1024 * 1024
        ),
    )(tokens, land_bits.reshape(count, 1, size), ocean_list, w_qkv, w_out, tables())


def solution(mesh):
    placed = (
        P(("groups", "lat", "lon"), None, None),
        P(("groups", "lat", "lon"), None),
        P(("groups", "lat"), None),
        P(None, None, None, "sub"),
        P(None, "sub", None),
    )
    return jax.shard_map(
        shards,
        mesh=mesh,
        in_specs=placed,
        out_specs=P(("groups", "lat", "lon"), None, None),
        check_vma=False,
    )
```
